32 devices in a mesh: dom: 16 (over z, x, core), feat: 2 (over y).
Axes of the slice: x: 2, y: 2, z: 4, core: 2. Of those that a mesh axis runs over, the one named last changes fastest.
Arguments:
- features: float32 [32768, 512], P('dom', 'feat'), may hold values from -6 to 6
- infill_mask: int32 [32768], P('dom'), may hold values 0 or 1
- mask_token: float32 [512], P('feat'), may hold values from -4 to 4
- local_rows: int32 [16, 64], P('dom'), may hold values from 0 to 15
- local_cols: int32 [16, 64], P('dom'), may hold values from 12 to 35, as said below
- local_tiles: float32 [16, 64, 128, 128], P('dom'), may hold values from -0.1875 to 0.1875
- hub_ids: int32 [512], P('dom'), may hold values from 0 to 32767, as said below
- hub_count: int32 [16], P('dom'), may hold values from 16 to 64, as said below
- hub_rows: int32 [16, 64], P('dom'), may hold values from 0 to 15
- hub_panels: int32 [16, 64], P('dom'), may hold values from 0 to 3
- hub_tiles: float32 [16, 64, 128, 128], P('dom'), may hold values from -0.1875 to 0.1875
- mix_weight: float32 [512, 512], P(None, 'feat'), may hold values from -0.25 to 0.25
- mix_bias: float32 [512], P('feat'), may hold values from -3 to 3
- norm_gain: float32 [512], P('feat'), may hold values from 0.25 to 1.75
Outputs:
- updated: float32 [32768, 512], P('dom', 'feat')
The draws below stay inside these ranges and needn't reach their ends.
Inputs may be any that keep to these rules, and one draw needn't show every extreme that they name: `hub_ids`: index block k of 32 entries holds distinct vertices of partition k. `hub_count`: some partition has all 64 slots live. `local_cols`: each local tile's column block differs from its row block plus 2048 // 128 by at most 4, and in every partition by exactly 4 on both sides.
All inputs are finite; a program needn't handle non-finite values. No bound on the sum of `infill_mask` on one device may be relied on, other than what follows from the above.
Results may differ from the reference program's by a relative error of at most 0.0003.
Values sent between devices are 32-bit elements; how exact they have to be, the bound alone decides.
A program may use at most 128 MiB of HBM per device.

```python
import jax
import jax.numpy as jnp
from jax import lax

D = 512
ROWS = 2048
LOC_TILES = 64
HUB_TILES = 64
HUB_DEV = 32
REACH = 4
VERTICES = 32768
HUBS = 512
N_DOM = 16


def local_layout(key):
    blocks = ROWS // 128
    rows_key = jax.random.fold_in(key, 31)
    offs_key = jax.random.fold_in(key, 32)
    row_blocks = jax.random.randint(rows_key, (N_DOM, LOC_TILES), 0, blocks)
    offsets = jax.random.randint(offs_key, (N_DOM, LOC_TILES), -REACH, REACH + 1)
    row_blocks = row_blocks.at[:, 0].set(0).at[:, 1].set(blocks - 1)
    offsets = offsets.at[:, 0].set(-REACH).at[:, 1].set(REACH)
    columns = row_blocks + blocks + offsets
    return (row_blocks.astype(jnp.int32), columns.astype(jnp.int32))


def draw_local_rows(key, part):
    return local_layout(key)[0]


def draw_local_cols(key, part):
    return local_layout(key)[1]


def draw_hub_ids(key, part):

    def owner_ids(owner):
        order = jax.random.permutation(jax.random.fold_in(key, owner), ROWS)[:HUB_DEV]
        return order.astype(jnp.int32) + owner * ROWS
    return jax.vmap(owner_ids)(jnp.arange(N_DOM, dtype=jnp.int32)).reshape(-1)


def draw_hub_count(key, part):
    counts = jax.random.randint(jax.random.fold_in(key, 11), (N_DOM,), HUB_TILES // 4, HUB_TILES + 1)
    fullest = jax.random.randint(jax.random.fold_in(key, 12), (), 0, N_DOM)
    return counts.at[fullest].set(HUB_TILES).astype(jnp.int32)


def set_ends(drawn, rng, least, top_value):
    index_at = [jax.random.randint(jax.random.fold_in(rng, axis), (), 0, length) for axis, length in enumerate(drawn.shape)]
    widest = drawn.shape.index(max(drawn.shape))
    next_to = index_at[:widest] + [(index_at[widest] + 1) % drawn.shape[widest]] + index_at[widest + 1:]
    return drawn.at[tuple(index_at)].set(least).at[tuple(next_to)].set(top_value)


def block_scale(stream_key, extent, pieces, least, largest):
    factor_of, own = 1.0, jax.random.fold_in(stream_key, 6)
    for dim, parts in pieces:
        heights = jnp.exp(jax.random.uniform(jax.random.fold_in(own, dim), (parts,), jnp.float32, least / len(pieces), largest / len(pieces)))
        factor_of = factor_of * jnp.repeat(heights, extent[dim] // parts).reshape([-1 if axis == dim else 1 for axis in range(len(extent))])
    return factor_of


def bell_draw(rng, dims, scale, reach, shards=(), held_as=jnp.bfloat16):
    values = scale * jax.random.normal(rng, dims, jnp.float32)
    if shards:
        values = values * block_scale(rng, dims, shards, -0.22, 0.18)
    return jnp.clip(values, -reach, reach).astype(held_as)


def setup_inputs(seed: int = 0) -> dict:
    key_of = jax.random.split(jax.random.key(seed), 15)
    return {
        "features": bell_draw(key_of[0], (VERTICES, D), 1.0, 6.0, ((0, 16), (1, 2)), jnp.float32),
        "infill_mask": set_ends((jax.random.randint(key_of[1], (VERTICES,), 0, 20) < 3).astype(jnp.int32), jax.random.fold_in(key_of[1], 1), 0, 1),
        "mask_token": bell_draw(key_of[2], (D,), 1.0, 4.0, ((0, 2),), jnp.float32),
        "local_rows": draw_local_rows(jax.random.fold_in(key_of[14], 71), 0),
        "local_cols": draw_local_cols(jax.random.fold_in(key_of[14], 71), 0),
        "local_tiles": bell_draw(key_of[5], (N_DOM, LOC_TILES, 128, 128), 1024 ** -0.5, 0.1875, ((0, 16),), jnp.float32),
        "hub_ids": draw_hub_ids(jax.random.fold_in(key_of[14], 71), 0),
        "hub_count": draw_hub_count(jax.random.fold_in(key_of[14], 71), 0),
        "hub_rows": set_ends(jax.random.randint(key_of[8], (N_DOM, HUB_TILES), 0, ROWS // 128), jax.random.fold_in(key_of[8], 1), 0, (ROWS // 128) - 1).astype(jnp.int32),
        "hub_panels": set_ends(jax.random.randint(key_of[9], (N_DOM, HUB_TILES), 0, HUBS // 128), jax.random.fold_in(key_of[9], 1), 0, (HUBS // 128) - 1).astype(jnp.int32),
        "hub_tiles": bell_draw(key_of[10], (N_DOM, HUB_TILES, 128, 128), 1024 ** -0.5, 0.1875, ((0, 16),), jnp.float32),
        "mix_weight": bell_draw(key_of[11], (D, D), D ** -0.5, 0.25, ((1, 2),), jnp.float32),
        "mix_bias": bell_draw(key_of[12], (D,), 0.5, 3.0, ((0, 2),), jnp.float32),
        "norm_gain": jnp.clip(1.0 + 0.15 * jax.random.normal(key_of[13], (D,), jnp.float32), 0.25, 1.75),
    }


def reference(features, infill_mask, mask_token, local_rows, local_cols, local_tiles, hub_ids, hub_count, hub_rows, hub_panels, hub_tiles, mix_weight, mix_bias, norm_gain):
    highest = lax.Precision.HIGHEST
    filled = jnp.where(infill_mask[:, None] == 1, mask_token[None, :], features)
    empty = jnp.zeros((ROWS, D), jnp.float32)
    padded = jnp.concatenate([empty, filled, empty], 0)
    panels = filled[hub_ids].reshape(HUBS // 128, 128, D)
    blocks = ROWS // 128
    block_ids = jnp.arange(blocks, dtype=jnp.int32)

    def partition(index):
        extended = lax.dynamic_slice_in_dim(padded, (index * ROWS).astype(jnp.int32), 3 * ROWS, 0)
        ext_blocks = extended.reshape(3 * blocks, 128, D)
        picked = ext_blocks[local_cols[index]]
        products = jnp.einsum('tij,tjf->tif', local_tiles[index], picked, precision=highest)
        row_onehot = (local_rows[index][None, :] == block_ids[:, None]).astype(jnp.float32)
        total = jnp.einsum('rt,tif->rif', row_onehot, products, precision=highest)
        hub_picked = panels[hub_panels[index]]
        hub_products = jnp.einsum('tij,tjf->tif', hub_tiles[index], hub_picked, precision=highest)
        live = (jnp.arange(HUB_TILES, dtype=jnp.int32) < hub_count[index]).astype(jnp.float32)
        hub_onehot = (hub_rows[index][None, :] == block_ids[:, None]).astype(jnp.float32) * live[None, :]
        total = total + jnp.einsum('rt,tif->rif', hub_onehot, hub_products, precision=highest)
        aggregate = total.reshape(ROWS, D)
        own = lax.dynamic_slice_in_dim(filled, (index * ROWS).astype(jnp.int32), ROWS, 0)
        pre = jnp.dot(aggregate, mix_weight, precision=highest) + mix_bias[None, :]
        hidden = own + jax.nn.silu(pre)
        mean_val = lax.optimization_barrier(jnp.sum(hidden, 1, keepdims=True)) / D
        square_val = lax.optimization_barrier(jnp.sum(hidden * hidden, 1, keepdims=True)) / D
        scale_val = lax.rsqrt(square_val - mean_val * mean_val + 1e-05)
        return (hidden - mean_val) * scale_val * norm_gain[None, :]
    result = lax.map(partition, jnp.arange(N_DOM, dtype=jnp.int32))
    return result.reshape(VERTICES, D)
```

```python
import functools

import jax
import jax.numpy as jnp
from jax import lax
from jax.experimental import pallas as pl
from jax.experimental.pallas import tpu as pltpu
from jax.sharding import PartitionSpec as P

REACH = 4
BLK = 128
F32 = jnp.float32
BF16 = jnp.bfloat16


def split(x):
    high = x.astype(BF16)
    low = (x - high.astype(F32)).astype(BF16)
    return high, low


def left_form(x):
    high, low = split(x)
    return jnp.concatenate([high, low, high], axis=1)


def right_form(x):
    high, low = split(x)
    return jnp.concatenate([high, high, low], axis=0)


def kernel(
    n,
    rows,
    half,
    hd,
    slots,
    tiles,
    chunk,
    feat_ref,
    mask_ref,
    token_ref,
    meta_ref,
    ltiles_ref,
    htiles_ref,
    w_ref,
    bias_ref,
    gain_ref,
    out_ref,
    fil,
    halo_lo,
    halo_hi,
    hubs,
    ext_b,
    hub_b,
    tl,
    sums,
    agg,
    other,
    hid,
    w_b,
    st_out,
    st_in,
    tile_sem,
    hub_send,
    hub_recv,
    halo_send,
    halo_recv,
    agg_send,
    agg_recv,
    st_send,
    st_recv,
    out_sem,
):
    blocks = rows // BLK
    panels = n * hd // BLK
    chunks = rows // chunk
    chips = n // 2
    me = lax.axis_index("dom")
    side = lax.axis_index("feat")
    core = lax.rem(me, 2)
    sibling = me + 1 - 2 * core
    halo = REACH * BLK

    barrier = pltpu.get_barrier_semaphore()

    def greet(j, _):
        pl.semaphore_signal(barrier, inc=1, device_id={"dom": lax.rem(me + j, n)})
        return 0

    lax.fori_loop(1, n, greet, 0)
    pl.semaphore_signal(barrier, inc=1, device_id={"feat": 1 - side})

    hub_tiles_copy = pltpu.make_async_copy(htiles_ref, tl.at[pl.ds(0, slots)], tile_sem.at[0])
    loc_tiles_copy = pltpu.make_async_copy(ltiles_ref, tl.at[pl.ds(slots, tiles)], tile_sem.at[1])
    hub_tiles_copy.start()
    loc_tiles_copy.start()

    token = token_ref[...]

    def fill(b, _):
        at = pl.ds(pl.multiple_of(b * BLK, BLK), BLK)
        flags = mask_ref[pl.ds(b, 1), :].astype(F32)
        turned = jnp.broadcast_to(flags, (BLK, BLK)).T
        wide = jnp.concatenate([turned] * (half // BLK), axis=1)
        got = jnp.where(wide == 1.0, jnp.broadcast_to(token, (BLK, half)), feat_ref[at, :])
        fil[at, :] = got
        ext_b[REACH + b] = right_form(got)
        return 0

    lax.fori_loop(0, blocks, fill, 0)

    ids_at = tiles + slots + tiles + slots + blocks
    base = me * hd

    def pick(i, _):
        hubs[pl.ds(base + i, 1), :] = fil[pl.ds(meta_ref[ids_at + i], 1), :]
        return 0

    lax.fori_loop(0, hd, pick, 0)

    pl.semaphore_wait(barrier, n)

    def hub_copy(owner, target, sem_at):
        at = pl.ds(pl.multiple_of(owner * hd, hd), hd)
        return pltpu.make_async_remote_copy(
            src_ref=hubs.at[at],
            dst_ref=hubs.at[at],
            send_sem=hub_send.at[sem_at],
            recv_sem=hub_recv.at[owner],
            device_id={"dom": target},
        )

    def send_far(j, _):
        hub_copy(me, lax.rem(me + 2 * j, n), j).start()
        return 0

    lax.fori_loop(1, chips, send_far, 0)
    hub_copy(me, sibling, 0).start()

    down = pltpu.make_async_remote_copy(
        src_ref=fil.at[pl.ds(0, halo)],
        dst_ref=halo_hi,
        send_sem=halo_send.at[0],
        recv_sem=halo_recv.at[0],
        device_id={"dom": lax.rem(me + n - 1, n)},
    )
    up = pltpu.make_async_remote_copy(
        src_ref=fil.at[pl.ds(rows - halo, halo)],
        dst_ref=halo_lo,
        send_sem=halo_send.at[1],
        recv_sem=halo_recv.at[1],
        device_id={"dom": lax.rem(me + 1, n)},
    )

    @pl.when(me > 0)
    def _():
        down.start()

    @pl.when(me < n - 1)
    def _():
        up.start()

    w_own = w_ref[pl.ds(pl.multiple_of(side * half, half), half), :]
    w_far = w_ref[pl.ds(pl.multiple_of((1 - side) * half, half), half), :]
    w_b[0] = right_form(w_own)
    w_b[1] = right_form(w_far)
    sums[0] = jnp.zeros((BLK, half), F32)

    def forward(j, _):
        owner = lax.rem(me + n - 2 * j, n)
        hub_copy(owner, sibling, 0).wait_recv()
        hub_copy(owner, sibling, chips + j).start()
        return 0

    lax.fori_loop(1, chips, forward, 0)

    def arrive(j, _):
        hub_copy(lax.rem(sibling + n - 2 * j, n), sibling, 0).wait_recv()
        return 0

    lax.fori_loop(0, chips, arrive, 0)

    def panel_form(p, _):
        hub_b[p] = right_form(hubs[pl.ds(pl.multiple_of(p * BLK, BLK), BLK), :])
        return 0

    lax.fori_loop(0, panels, panel_form, 0)
    hub_tiles_copy.wait()

    chain_at = tiles + slots
    group = 4

    def hub_products(g, _):
        for u in range(group):
            t = g * group + u
            got = jnp.dot(left_form(tl[t]), hub_b[meta_ref[tiles + t]], preferred_element_type=F32)
            sums[t + 1] = got + sums[meta_ref[chain_at + t]]
        return 0

    lax.fori_loop(0, slots // group, hub_products, 0)

    @pl.when(me > 0)
    def _():
        up.wait_recv()

    @pl.when(me == 0)
    def _():
        halo_lo[...] = jnp.zeros((halo, half), F32)

    @pl.when(me < n - 1)
    def _():
        down.wait_recv()

    @pl.when(me == n - 1)
    def _():
        halo_hi[...] = jnp.zeros((halo, half), F32)

    for b in range(REACH):
        ext_b[b] = right_form(halo_lo[pl.ds(b * BLK, BLK), :])
        ext_b[REACH + blocks + b] = right_form(halo_hi[pl.ds(b * BLK, BLK), :])
    loc_tiles_copy.wait()

    def loc_products(g, _):
        for u in range(group):
            t = g * group + u
            got = jnp.dot(left_form(tl[slots + t]), ext_b[meta_ref[t]], preferred_element_type=F32)
            sums[slots + t + 1] = got + sums[meta_ref[chain_at + slots + t]]
        return 0

    lax.fori_loop(0, tiles // group, loc_products, 0)

    last_at = chain_at + slots + tiles
    per = chunk // BLK

    def chunk_rows(c):
        return pl.ds(pl.multiple_of(c * chunk, chunk), chunk)

    def agg_copy(c):
        return pltpu.make_async_remote_copy(
            src_ref=agg.at[chunk_rows(c)],
            dst_ref=other.at[chunk_rows(c)],
            send_sem=agg_send.at[c],
            recv_sem=agg_recv.at[c],
            device_id={"feat": 1 - side},
        )

    def st_copy(c):
        return pltpu.make_async_remote_copy(
            src_ref=st_out.at[c],
            dst_ref=st_in.at[c],
            send_sem=st_send.at[c],
            recv_sem=st_recv.at[c],
            device_id={"feat": 1 - side},
        )

    def out_copy(c):
        return pltpu.make_async_copy(hid.at[chunk_rows(c)], out_ref.at[chunk_rows(c)], out_sem.at[c])

    def send_chunk(c, _):
        for u in range(per):
            r = c * per + u
            agg[pl.ds(pl.multiple_of(r * BLK, BLK), BLK), :] = sums[meta_ref[last_at + r]]
        agg_copy(c).start()
        return 0

    lax.fori_loop(0, chunks, send_chunk, 0)

    bias = bias_ref[...]
    gain = gain_ref[...]
    width = 2.0 * half

    def finish(c):
        st_copy(c).wait_recv()
        both = st_out[c] + st_in[c]
        turned = jnp.concatenate([both] * (BLK // 8), axis=0).T
        mean = turned[:, 0:1] / width
        square = turned[:, 4:5] / width
        scale = lax.rsqrt(square - mean * mean + 1e-05)
        hid[chunk_rows(c), :] = (hid[chunk_rows(c), :] - mean) * scale * gain
        out_copy(c).start()

    def mix(c, _):
        at = chunk_rows(c)
        pre = jnp.dot(left_form(agg[at, :]), w_b[0], preferred_element_type=F32)
        agg_copy(c).wait_recv()
        pre = pre + jnp.dot(left_form(other[at, :]), w_b[1], preferred_element_type=F32) + bias
        hidden = fil[at, :] + pre / (1.0 + jnp.exp(-pre))
        hid[at, :] = hidden
        one = jnp.sum(hidden, axis=1, keepdims=True)
        two = jnp.sum(hidden * hidden, axis=1, keepdims=True)
        lane = lax.broadcasted_iota(jnp.int32, (chunk, BLK), 1)
        packed = jnp.where(lax.rem(lane, 8) < 4, jnp.broadcast_to(one, (chunk, BLK)), jnp.broadcast_to(two, (chunk, BLK)))
        st_out[c] = packed.T[0:8, :]
        st_copy(c).start()

        @pl.when(c > 0)
        def _():
            finish(c - 1)

        return 0

    lax.fori_loop(0, chunks, mix, 0)
    finish(chunks - 1)

    def close(c, _):
        agg_copy(c).wait_send()
        st_copy(c).wait_send()
        out_copy(c).wait()
        return 0

    lax.fori_loop(0, chunks, close, 0)

    def close_far(j, _):
        hub_copy(me, sibling, j).wait_send()
        hub_copy(me, sibling, chips + j).wait_send()
        return 0

    lax.fori_loop(1, chips, close_far, 0)
    hub_copy(me, sibling, 0).wait_send()

    @pl.when(me > 0)
    def _():
        down.wait_send()

    @pl.when(me < n - 1)
    def _():
        up.wait_send()


def shards(
    features,
    infill_mask,
    mask_token,
    local_rows,
    local_cols,
    local_tiles,
    hub_ids,
    hub_count,
    hub_rows,
    hub_panels,
    hub_tiles,
    mix_weight,
    mix_bias,
    norm_gain,
):
    rows, half = features.shape
    blocks = rows // BLK
    n = lax.axis_size("dom")
    hd = hub_ids.shape[0]
    tiles = local_rows.shape[1]
    slots = hub_rows.shape[1]
    chunk = 256
    chunks = rows // chunk
    i32 = jnp.int32

    live = jnp.arange(slots, dtype=i32) < hub_count[0]
    row_of = jnp.concatenate([jnp.where(live, hub_rows[0], -1), local_rows[0]])
    total = slots + tiles
    seq = jnp.arange(total, dtype=i32)
    target = jnp.concatenate([row_of, jnp.arange(blocks, dtype=i32)])
    limit = jnp.concatenate([seq, jnp.full((blocks,), total, i32)])
    same = (row_of[None, :] == target[:, None]) & (seq[None, :] < limit[:, None])
    chain = jnp.max(jnp.where(same, seq[None, :] + 1, 0), axis=1)
    meta = jnp.concatenate(
        [
            local_cols[0] - (blocks - REACH),
            hub_panels[0],
            chain,
            hub_ids - lax.axis_index("dom") * rows,
        ]
    )

    vmem = pl.BlockSpec(memory_space=pltpu.VMEM)
    smem = pl.BlockSpec(memory_space=pltpu.SMEM)
    anym = pl.BlockSpec(memory_space=pl.ANY)
    dma = pltpu.SemaphoreType.DMA
    flops = 6 * BLK * BLK * half * total + 6 * rows * 2 * half * half
    return pl.pallas_call(
        functools.partial(kernel, n, rows, half, hd, slots, tiles, chunk),
        out_shape=jax.ShapeDtypeStruct((rows, half), F32),
        in_specs=[vmem, vmem, vmem, smem, anym, anym, vmem, vmem, vmem],
        out_specs=anym,
        scratch_shapes=[
            pltpu.VMEM((rows, half), F32),
            pltpu.VMEM((REACH * BLK, half), F32),
            pltpu.VMEM((REACH * BLK, half), F32),
            pltpu.VMEM((n * hd, half), F32),
            pltpu.VMEM((blocks + 2 * REACH, 3 * BLK, half), BF16),
            pltpu.VMEM((n * hd // BLK, 3 * BLK, half), BF16),
            pltpu.VMEM((total, BLK, BLK), F32),
            pltpu.VMEM((total + 1, BLK, half), F32),
            pltpu.VMEM((rows, half), F32),
            pltpu.VMEM((rows, half), F32),
            pltpu.VMEM((rows, half), F32),
            pltpu.VMEM((2, 3 * half, half), BF16),
            pltpu.VMEM((chunks, 8, chunk), F32),
            pltpu.VMEM((chunks, 8, chunk), F32),
            dma((2,)),
            dma((n,)),
            dma((n,)),
            dma((2,)),
            dma((2,)),
            dma((chunks,)),
            dma((chunks,)),
            dma((chunks,)),
            dma((chunks,)),
            dma((chunks,)),
        ],
        compiler_params=pltpu.CompilerParams(
            collective_id=0, has_side_effects=True, vmem_limit_bytes=58 * 1024 * 1024
        ),
        cost_estimate=pl.CostEstimate(flops=flops, bytes_accessed=13 << 20, transcendentals=rows * half),
    )(
        features,
        infill_mask.reshape(blocks, BLK),
        mask_token[None, :],
        meta,
        local_tiles[0],
        hub_tiles[0],
        mix_weight,
        mix_bias[None, :],
        norm_gain[None, :],
    )


def solution(mesh):
    in_specs = (
        P("dom", "feat"),
        P("dom"),
        P("feat"),
        P("dom", None),
        P("dom", None),
        P("dom", None, None, None),
        P("dom"),
        P("dom"),
        P("dom", None),
        P("dom", None),
        P("dom", None, None, None),
        P(None, "feat"),
        P("feat"),
        P("feat"),
    )
    out_specs = P("dom", "feat")
    return jax.shard_map(shards, mesh=mesh, in_specs=in_specs, out_specs=out_specs, check_vma=False)
```

```python
import functools

import jax
import jax.numpy as jnp
from jax import lax
from jax.experimental import pallas as pl
from jax.experimental.pallas import tpu as pltpu
from jax.sharding import PartitionSpec as P

REACH = 4
BLK = 128
F32 = jnp.float32
BF16 = jnp.bfloat16


def split(x):
    high = x.astype(BF16)
    low = (x - high.astype(F32)).astype(BF16)
    return high, low


def left_form(x):
    high, low = split(x)
    return jnp.concatenate([high, low, high], axis=1)


def right_form(x):
    high, low = split(x)
    return jnp.concatenate([high, high, low], axis=0)


def kernel(
    n,
    rows,
    half,
    hd,
    slots,
    tiles,
    chunk,
    feat_ref,
    mask_ref,
    token_ref,
    cols_ref,
    panels_ref,
    ids_ref,
    chain_ref,
    ltiles_ref,
    htiles_ref,
    w_ref,
    bias_ref,
    out_ref,
    fil,
    halo_lo,
    halo_hi,
    early,
    early_in,
    early_lo,
    early_hi,
    hub_out,
    hub_in,
    hubs,
    ext_b,
    hub_b,
    tl,
    sums,
    agg,
    late,
    late_in,
    hid,
    w_b,
    st_out,
    st_in,
    tile_sem,
    feat_sem,
    early_send,
    early_recv,
    hop_send,
    hop_recv,
    hub_send,
    hub_recv,
    halo_send,
    halo_recv,
    agg_send,
    agg_recv,
    st_send,
    st_recv,
    out_sem,
):
    blocks = rows // BLK
    panels = n * hd // BLK
    chunks = rows // chunk
    chips = n // 2
    me = lax.axis_index("dom")
    side = lax.axis_index("feat")
    core = lax.rem(me, 2)
    sibling = me + 1 - 2 * core
    halo = REACH * BLK
    part = half // 2
    pieces = rows // halo
    mate = {"feat": 1 - side}

    feat_copies = [
        pltpu.make_async_copy(feat_ref.at[pl.ds(q * halo, halo)], fil.at[pl.ds(q * halo, halo)], feat_sem.at[q])
        for q in range(pieces)
    ]
    for copy in feat_copies:
        copy.start()

    barrier = pltpu.get_barrier_semaphore()

    def greet(j, _):
        pl.semaphore_signal(barrier, inc=1, device_id={"dom": lax.rem(me + j, n)})
        return 0

    lax.fori_loop(1, n, greet, 0)
    pl.semaphore_signal(barrier, inc=1, device_id={"feat": 1 - side})

    hub_tiles_copy = pltpu.make_async_copy(htiles_ref, tl.at[pl.ds(0, slots)], tile_sem.at[0])
    loc_tiles_copy = pltpu.make_async_copy(ltiles_ref, tl.at[pl.ds(slots, tiles)], tile_sem.at[1])
    hub_tiles_copy.start()
    loc_tiles_copy.start()

    token = token_ref[...]

    def fill(b, _):
        at = pl.ds(pl.multiple_of(b * BLK, BLK), BLK)
        flags = mask_ref[pl.ds(b, 1), :].astype(F32)
        turned = jnp.broadcast_to(flags, (BLK, BLK)).T
        wide = jnp.concatenate([turned] * (half // BLK), axis=1)
        got = jnp.where(wide == 1.0, jnp.broadcast_to(token, (BLK, half)), fil[at, :])
        fil[at, :] = got
        early[at, :] = got[:, part:]
        ext_b[REACH + b] = right_form(got)
        return 0

    for q in range(pieces):
        feat_copies[q].wait()
        lax.fori_loop(q * REACH, (q + 1) * REACH, fill, 0)

    base = pl.multiple_of(me * hd, hd)
    first = me * rows

    def pick(i, _):
        got = fil[pl.ds(jnp.maximum(ids_ref[i] - first, 0), 1), :]
        hubs[pl.ds(base + i, 1), 0:half] = got
        hub_out[pl.ds(i, 1), :] = got[:, part:]
        return 0

    lax.fori_loop(0, hd, pick, 0)

    pl.semaphore_wait(barrier, n)

    hop = pltpu.make_async_remote_copy(
        src_ref=hub_out,
        dst_ref=hub_in,
        send_sem=hop_send.at[0],
        recv_sem=hop_recv.at[0],
        device_id=mate,
    )
    hop.start()

    def early_copy(q):
        at = pl.ds(q * halo, halo)
        return pltpu.make_async_remote_copy(
            src_ref=early.at[at],
            dst_ref=early_in.at[at],
            send_sem=early_send.at[q],
            recv_sem=early_recv.at[q],
            device_id=mate,
        )

    order = [0, pieces - 1] + list(range(1, pieces - 1))
    for q in order:
        early_copy(q).start()

    def hub_copy(owner, target, sem_at):
        at = pl.ds(pl.multiple_of(owner * hd, hd), hd)
        return pltpu.make_async_remote_copy(
            src_ref=hubs.at[at],
            dst_ref=hubs.at[at],
            send_sem=hub_send.at[sem_at],
            recv_sem=hub_recv.at[owner],
            device_id={"dom": target},
        )

    hop.wait_recv()
    hubs[pl.ds(base, hd), half:] = hub_in[...]

    def send_far(j, _):
        hub_copy(me, lax.rem(me + 2 * j, n), j).start()
        return 0

    lax.fori_loop(1, chips, send_far, 0)
    hub_copy(me, sibling, 0).start()

    down = pltpu.make_async_remote_copy(
        src_ref=fil.at[pl.ds(0, halo)],
        dst_ref=halo_hi,
        send_sem=halo_send.at[0],
        recv_sem=halo_recv.at[0],
        device_id={"dom": lax.rem(me + n - 1, n)},
    )
    up = pltpu.make_async_remote_copy(
        src_ref=fil.at[pl.ds(rows - halo, halo)],
        dst_ref=halo_lo,
        send_sem=halo_send.at[1],
        recv_sem=halo_recv.at[1],
        device_id={"dom": lax.rem(me + 1, n)},
    )

    @pl.when(me > 0)
    def _():
        down.start()

    @pl.when(me < n - 1)
    def _():
        up.start()

    early_down = pltpu.make_async_remote_copy(
        src_ref=early_in.at[pl.ds(0, halo)],
        dst_ref=early_hi,
        send_sem=halo_send.at[2],
        recv_sem=halo_recv.at[2],
        device_id={"dom": lax.rem(me + n - 1, n)},
    )
    early_up = pltpu.make_async_remote_copy(
        src_ref=early_in.at[pl.ds(rows - halo, halo)],
        dst_ref=early_lo,
        send_sem=halo_send.at[3],
        recv_sem=halo_recv.at[3],
        device_id={"dom": lax.rem(me + 1, n)},
    )

    w_own = w_ref[pl.ds(pl.multiple_of(side * half, half), half), :]
    w_far = w_ref[pl.ds(pl.multiple_of((1 - side) * half, half), half), :]
    w_b[pl.ds(0, 3 * half), :] = right_form(w_own)
    w_b[pl.ds(3 * half, 3 * part), :] = right_form(w_far[part:, :])
    w_b[pl.ds(3 * half + 3 * part, 3 * part), :] = right_form(w_far[:part, :])
    sums[0] = jnp.zeros((BLK, half), F32)

    def forward(j, _):
        owner = lax.rem(me + n - 2 * j, n)
        hub_copy(owner, sibling, 0).wait_recv()
        hub_copy(owner, sibling, chips + j).start()
        return 0

    lax.fori_loop(1, chips, forward, 0)

    def arrive(j, _):
        hub_copy(lax.rem(sibling + n - 2 * j, n), sibling, 0).wait_recv()
        return 0

    lax.fori_loop(0, chips, arrive, 0)

    def panel_form(p, _):
        hub_b[p] = right_form(hubs[pl.ds(pl.multiple_of(p * BLK, BLK), BLK), 0:half])
        return 0

    lax.fori_loop(0, panels, panel_form, 0)
    hub_tiles_copy.wait()

    last_at = slots + tiles
    shift = blocks - REACH
    group = 4

    def hub_products(g, _):
        for u in range(group):
            t = g * group + u
            got = jnp.dot(left_form(tl[t]), hub_b[panels_ref[0, t]], preferred_element_type=F32)
            sums[t + 1] = got + sums[chain_ref[t]]
        return 0

    lax.fori_loop(0, slots // group, hub_products, 0)

    early_copy(0).wait_recv()
    early_copy(pieces - 1).wait_recv()

    @pl.when(me > 0)
    def _():
        early_down.start()

    @pl.when(me < n - 1)
    def _():
        early_up.start()

    @pl.when(me > 0)
    def _():
        up.wait_recv()

    @pl.when(me == 0)
    def _():
        halo_lo[...] = jnp.zeros((halo, half), F32)

    @pl.when(me < n - 1)
    def _():
        down.wait_recv()

    @pl.when(me == n - 1)
    def _():
        halo_hi[...] = jnp.zeros((halo, half), F32)

    for b in range(REACH):
        ext_b[b] = right_form(halo_lo[pl.ds(b * BLK, BLK), :])
        ext_b[REACH + blocks + b] = right_form(halo_hi[pl.ds(b * BLK, BLK), :])
    loc_tiles_copy.wait()

    def loc_products(g, _):
        for u in range(group):
            t = g * group + u
            got = jnp.dot(left_form(tl[slots + t]), ext_b[jnp.maximum(cols_ref[0, t] - shift, 0)], preferred_element_type=F32)
            sums[slots + t + 1] = got + sums[chain_ref[slots + t]]
        return 0

    lax.fori_loop(0, tiles // group, loc_products, 0)

    per = chunk // BLK

    def chunk_rows(c):
        return pl.ds(pl.multiple_of(c * chunk, chunk), chunk)

    def agg_copy(c):
        return pltpu.make_async_remote_copy(
            src_ref=late.at[chunk_rows(c)],
            dst_ref=late_in.at[chunk_rows(c)],
            send_sem=agg_send.at[c],
            recv_sem=agg_recv.at[c],
            device_id=mate,
        )

    def st_copy(c):
        return pltpu.make_async_remote_copy(
            src_ref=st_out.at[c],
            dst_ref=st_in.at[c],
            send_sem=st_send.at[c],
            recv_sem=st_recv.at[c],
            device_id=mate,
        )

    def out_copy(c):
        return pltpu.make_async_copy(hid.at[chunk_rows(c)], out_ref.at[chunk_rows(c)], out_sem.at[c])

    def send_chunk(c, _):
        for u in range(per):
            r = c * per + u
            at = pl.ds(pl.multiple_of(r * BLK, BLK), BLK)
            got = sums[chain_ref[last_at + r]]
            agg[at, :] = got
            late[at, :] = got[:, :part]
        agg_copy(c).start()
        return 0

    lax.fori_loop(0, chunks, send_chunk, 0)

    def hub_early(p, _):
        hub_b[p, :, 0:part] = right_form(hubs[pl.ds(pl.multiple_of(p * BLK, BLK), BLK), half:])
        return 0

    lax.fori_loop(0, panels, hub_early, 0)

    def hub_products_early(g, _):
        for u in range(group):
            t = g * group + u
            right = hub_b[panels_ref[0, t], :, 0:part]
            got = jnp.dot(left_form(tl[t]), right, preferred_element_type=F32)
            sums[t + 1, :, 0:part] = got + sums[chain_ref[t], :, 0:part]
        return 0

    lax.fori_loop(0, slots // group, hub_products_early, 0)

    for q in range(1, pieces - 1):
        early_copy(q).wait_recv()

    def own_early(b, _):
        ext_b[REACH + b, :, 0:part] = right_form(early_in[pl.ds(pl.multiple_of(b * BLK, BLK), BLK), :])
        return 0

    lax.fori_loop(0, blocks, own_early, 0)

    @pl.when(me > 0)
    def _():
        early_up.wait_recv()

    @pl.when(me == 0)
    def _():
        early_lo[...] = jnp.zeros((halo, part), F32)

    @pl.when(me < n - 1)
    def _():
        early_down.wait_recv()

    @pl.when(me == n - 1)
    def _():
        early_hi[...] = jnp.zeros((halo, part), F32)

    for b in range(REACH):
        ext_b[b, :, 0:part] = right_form(early_lo[pl.ds(b * BLK, BLK), :])
        ext_b[REACH + blocks + b, :, 0:part] = right_form(early_hi[pl.ds(b * BLK, BLK), :])

    def loc_products_early(g, _):
        for u in range(group):
            t = g * group + u
            right = ext_b[jnp.maximum(cols_ref[0, t] - shift, 0), :, 0:part]
            got = jnp.dot(left_form(tl[slots + t]), right, preferred_element_type=F32)
            sums[slots + t + 1, :, 0:part] = got + sums[chain_ref[slots + t], :, 0:part]
        return 0

    lax.fori_loop(0, tiles // group, loc_products_early, 0)

    bias = bias_ref[...]
    width = 2.0 * half

    def finish(c):
        st_copy(c).wait_recv()
        both = st_out[c] + st_in[c]
        turned = jnp.concatenate([both] * (BLK // 8), axis=0).T
        mean = turned[:, 0:1] / width
        square = turned[:, 4:5] / width
        scale = lax.rsqrt(square - mean * mean + 1e-05)
        hid[chunk_rows(c), :] = (hid[chunk_rows(c), :] - mean) * scale
        out_copy(c).start()

    def mix(c, _):
        at = chunk_rows(c)
        got = jnp.concatenate([sums[chain_ref[last_at + c * per + u], :, 0:part] for u in range(per)], axis=0)
        left = jnp.concatenate([left_form(agg[at, :]), left_form(got)], axis=1)
        pre = jnp.dot(left, w_b[pl.ds(0, 3 * half + 3 * part), :], preferred_element_type=F32) + bias
        agg_copy(c).wait_recv()
        right = w_b[pl.ds(3 * half + 3 * part, 3 * part), :]
        pre = pre + jnp.dot(left_form(late_in[at, :]), right, preferred_element_type=F32)
        hidden = fil[at, :] + pre / (1.0 + jnp.exp(-pre))
        hid[at, :] = hidden
        one = jnp.sum(hidden, axis=1, keepdims=True)
        two = jnp.sum(hidden * hidden, axis=1, keepdims=True)
        lane = lax.broadcasted_iota(jnp.int32, (chunk, BLK), 1)
        packed = jnp.where(lax.rem(lane, 8) < 4, jnp.broadcast_to(one, (chunk, BLK)), jnp.broadcast_to(two, (chunk, BLK)))
        st_out[c] = packed.T[0:8, :]
        st_copy(c).start()

        @pl.when(c > 0)
        def _():
            finish(c - 1)

        return 0

    lax.fori_loop(0, chunks, mix, 0)
    finish(chunks - 1)

    def close(c, _):
        agg_copy(c).wait_send()
        st_copy(c).wait_send()
        out_copy(c).wait()
        return 0

    lax.fori_loop(0, chunks, close, 0)

    def close_far(j, _):
        hub_copy(me, sibling, j).wait_send()
        hub_copy(me, sibling, chips + j).wait_send()
        return 0

    lax.fori_loop(1, chips, close_far, 0)
    hop.wait_send()
    for q in range(pieces):
        early_copy(q).wait_send()
    hub_copy(me, sibling, 0).wait_send()

    @pl.when(me > 0)
    def _():
        down.wait_send()
        early_down.wait_send()

    @pl.when(me < n - 1)
    def _():
        up.wait_send()
        early_up.wait_send()


def shards(
    features,
    infill_mask,
    mask_token,
    local_rows,
    local_cols,
    local_tiles,
    hub_ids,
    hub_count,
    hub_rows,
    hub_panels,
    hub_tiles,
    mix_weight,
    mix_bias,
    norm_gain,
):
    rows, half = features.shape
    blocks = rows // BLK
    n = lax.axis_size("dom")
    hd = hub_ids.shape[0]
    tiles = local_rows.shape[1]
    slots = hub_rows.shape[1]
    chunk = 256
    chunks = rows // chunk
    i32 = jnp.int32

    live = jnp.arange(slots, dtype=i32) < hub_count[0]
    row_of = jnp.concatenate([jnp.where(live, hub_rows[0], -1), local_rows[0]])
    total = slots + tiles
    seq = jnp.arange(total, dtype=i32)
    target = jnp.concatenate([row_of, jnp.arange(blocks, dtype=i32)])
    limit = jnp.concatenate([seq, jnp.full((blocks,), total, i32)])
    same = (row_of[None, :] == target[:, None]) & (seq[None, :] < limit[:, None])
    chain = jnp.max(jnp.where(same, seq[None, :] + 1, 0), axis=1)

    vmem = pl.BlockSpec(memory_space=pltpu.VMEM)
    smem = pl.BlockSpec(memory_space=pltpu.SMEM)
    anym = pl.BlockSpec(memory_space=pl.ANY)
    dma = pltpu.SemaphoreType.DMA
    flops = 6 * BLK * BLK * half * total + 6 * rows * 2 * half * half
    part = half // 2
    halo = REACH * BLK
    pieces = rows // halo
    normed = pl.pallas_call(
        functools.partial(kernel, n, rows, half, hd, slots, tiles, chunk),
        out_shape=jax.ShapeDtypeStruct((rows, half), F32),
        in_specs=[anym, vmem, vmem, smem, smem, smem, smem, anym, anym, vmem, vmem],
        out_specs=anym,
        scratch_shapes=[
            pltpu.VMEM((rows, half), F32),
            pltpu.VMEM((REACH * BLK, half), F32),
            pltpu.VMEM((REACH * BLK, half), F32),
            pltpu.VMEM((rows, part), F32),
            pltpu.VMEM((rows, part), F32),
            pltpu.VMEM((halo, part), F32),
            pltpu.VMEM((halo, part), F32),
            pltpu.VMEM((hd, part), F32),
            pltpu.VMEM((hd, part), F32),
            pltpu.VMEM((n * hd, half + part), F32),
            pltpu.VMEM((blocks + 2 * REACH, 3 * BLK, half), BF16),
            pltpu.VMEM((n * hd // BLK, 3 * BLK, half), BF16),
            pltpu.VMEM((total, BLK, BLK), F32),
            pltpu.VMEM((total + 1, BLK, half), F32),
            pltpu.VMEM((rows, half), F32),
            pltpu.VMEM((rows, part), F32),
            pltpu.VMEM((rows, part), F32),
            pltpu.VMEM((rows, half), F32),
            pltpu.VMEM((6 * half, half), BF16),
            pltpu.VMEM((chunks, 8, chunk), F32),
            pltpu.VMEM((chunks, 8, chunk), F32),
            dma((2,)),
            dma((pieces,)),
            dma((pieces,)),
            dma((pieces,)),
            dma((1,)),
            dma((1,)),
            dma((n,)),
            dma((n,)),
            dma((4,)),
            dma((4,)),
            dma((chunks,)),
            dma((chunks,)),
            dma((chunks,)),
            dma((chunks,)),
            dma((chunks,)),
        ],
        compiler_params=pltpu.CompilerParams(
            collective_id=0, has_side_effects=True, vmem_limit_bytes=58 * 1024 * 1024
        ),
        cost_estimate=pl.CostEstimate(flops=flops, bytes_accessed=13 << 20, transcendentals=rows * half),
    )(
        features,
        infill_mask.reshape(blocks, BLK),
        mask_token[None, :],
        local_cols,
        hub_panels,
        hub_ids,
        chain,
        local_tiles[0],
        hub_tiles[0],
        mix_weight,
        mix_bias[None, :],
    )
    return normed * norm_gain[None, :]


def solution(mesh):
    in_specs = (
        P("dom", "feat"),
        P("dom"),
        P("feat"),
        P("dom", None),
        P("dom", None),
        P("dom", None, None, None),
        P("dom"),
        P("dom"),
        P("dom", None),
        P("dom", None),
        P("dom", None, None, None),
        P(None, "feat"),
        P("feat"),
        P("feat"),
    )
    out_specs = P("dom", "feat")
    return jax.shard_map(shards, mesh=mesh, in_specs=in_specs, out_specs=out_specs, check_vma=False)
```

```python
import functools

import jax
import jax.numpy as jnp
from jax import lax
from jax.experimental import pallas as pl
from jax.experimental.pallas import tpu as pltpu
from jax.sharding import PartitionSpec as P

REACH = 4
BLK = 128
F32 = jnp.float32
BF16 = jnp.bfloat16


def split(x):
    high = x.astype(BF16)
    low = (x - high.astype(F32)).astype(BF16)
    return high, low


def left_form(x):
    high, low = split(x)
    return jnp.concatenate([high, low, high], axis=1)


def right_form(x):
    high, low = split(x)
    return jnp.concatenate([high, high, low], axis=0)


def kernel(
    n,
    rows,
    half,
    hd,
    slots,
    tiles,
    chunk,
    feat_ref,
    mask_ref,
    token_ref,
    cols_ref,
    panels_ref,
    ids_ref,
    chain_ref,
    ltiles_ref,
    htiles_ref,
    w_ref,
    bias_ref,
    out_ref,
    fil,
    halo_lo,
    halo_hi,
    early,
    early_in,
    early_lo,
    early_hi,
    hub_out,
    hub_in,
    hubs,
    hubs_early,
    ext_b,
    hub_b,
    tl,
    sums,
    agg,
    late,
    late_in,
    hid,
    w_b,
    st_out,
    st_in,
    tile_sem,
    feat_sem,
    early_send,
    early_recv,
    hop_send,
    hop_recv,
    hub_send,
    hub_recv,
    hub_early_send,
    hub_early_recv,
    halo_send,
    halo_recv,
    agg_send,
    agg_recv,
    st_send,
    st_recv,
    out_sem,
):
    blocks = rows // BLK
    panels = n * hd // BLK
    chunks = rows // chunk
    chips = n // 2
    me = lax.axis_index("dom")
    side = lax.axis_index("feat")
    core = lax.rem(me, 2)
    sibling = me + 1 - 2 * core
    halo = REACH * BLK
    part = half // 2
    pieces = rows // halo
    mate = {"feat": 1 - side}

    feat_copies = [
        pltpu.make_async_copy(feat_ref.at[pl.ds(q * halo, halo)], fil.at[pl.ds(q * halo, halo)], feat_sem.at[q])
        for q in range(pieces)
    ]
    for copy in feat_copies:
        copy.start()

    barrier = pltpu.get_barrier_semaphore()

    def greet(j, _):
        pl.semaphore_signal(barrier, inc=1, device_id={"dom": lax.rem(me + j, n)})
        return 0

    lax.fori_loop(1, n, greet, 0)
    pl.semaphore_signal(barrier, inc=1, device_id={"feat": 1 - side})

    hub_tiles_copy = pltpu.make_async_copy(htiles_ref, tl.at[pl.ds(0, slots)], tile_sem.at[0])
    loc_tiles_copy = pltpu.make_async_copy(ltiles_ref, tl.at[pl.ds(slots, tiles)], tile_sem.at[1])
    hub_tiles_copy.start()
    loc_tiles_copy.start()

    token = token_ref[...]

    def fill(b, _):
        at = pl.ds(pl.multiple_of(b * BLK, BLK), BLK)
        flags = mask_ref[pl.ds(b, 1), :].astype(F32)
        turned = jnp.broadcast_to(flags, (BLK, BLK)).T
        wide = jnp.concatenate([turned] * (half // BLK), axis=1)
        got = jnp.where(wide == 1.0, jnp.broadcast_to(token, (BLK, half)), fil[at, :])
        fil[at, :] = got
        early[at, :] = got[:, part:]
        ext_b[REACH + b] = right_form(got)
        return 0

    for q in range(pieces):
        feat_copies[q].wait()
        lax.fori_loop(q * REACH, (q + 1) * REACH, fill, 0)

    base = pl.multiple_of(me * hd, hd)
    first = me * rows

    def pick(i, _):
        got = fil[pl.ds(jnp.maximum(ids_ref[i] - first, 0), 1), :]
        hubs[pl.ds(base + i, 1), :] = got
        hub_out[pl.ds(i, 1), :] = got[:, part:]
        return 0

    lax.fori_loop(0, hd, pick, 0)

    pl.semaphore_wait(barrier, n)

    def copies_of(buffer, sends, recvs):
        def hub_copy(owner, target, sem_at):
            at = pl.ds(pl.multiple_of(owner * hd, hd), hd)
            return pltpu.make_async_remote_copy(
                src_ref=buffer.at[at],
                dst_ref=buffer.at[at],
                send_sem=sends.at[sem_at],
                recv_sem=recvs.at[owner],
                device_id={"dom": target},
            )

        return hub_copy

    def send_own(hub_copy):
        def send_far(j, _):
            hub_copy(me, lax.rem(me + 2 * j, n), j).start()
            return 0

        lax.fori_loop(1, chips, send_far, 0)
        hub_copy(me, sibling, 0).start()

    def pass_on(hub_copy):
        def forward(j, _):
            owner = lax.rem(me + n - 2 * j, n)
            hub_copy(owner, sibling, 0).wait_recv()
            hub_copy(owner, sibling, chips + j).start()
            return 0

        lax.fori_loop(1, chips, forward, 0)

    def await_sibling(hub_copy):
        def arrive(j, _):
            hub_copy(lax.rem(sibling + n - 2 * j, n), sibling, 0).wait_recv()
            return 0

        lax.fori_loop(0, chips, arrive, 0)

    def close_sends(hub_copy):
        def close_far(j, _):
            hub_copy(me, sibling, j).wait_send()
            hub_copy(me, sibling, chips + j).wait_send()
            return 0

        lax.fori_loop(1, chips, close_far, 0)
        hub_copy(me, sibling, 0).wait_send()

    main_copy = copies_of(hubs, hub_send, hub_recv)
    side_copy = copies_of(hubs_early, hub_early_send, hub_early_recv)
    send_own(main_copy)

    hop = pltpu.make_async_remote_copy(
        src_ref=hub_out,
        dst_ref=hub_in,
        send_sem=hop_send.at[0],
        recv_sem=hop_recv.at[0],
        device_id=mate,
    )
    hop.start()

    def early_copy(q):
        at = pl.ds(q * halo, halo)
        return pltpu.make_async_remote_copy(
            src_ref=early.at[at],
            dst_ref=early_in.at[at],
            send_sem=early_send.at[q],
            recv_sem=early_recv.at[q],
            device_id=mate,
        )

    order = [0, pieces - 1] + list(range(1, pieces - 1))
    for q in order:
        early_copy(q).start()

    down = pltpu.make_async_remote_copy(
        src_ref=fil.at[pl.ds(0, halo)],
        dst_ref=halo_hi,
        send_sem=halo_send.at[0],
        recv_sem=halo_recv.at[0],
        device_id={"dom": lax.rem(me + n - 1, n)},
    )
    up = pltpu.make_async_remote_copy(
        src_ref=fil.at[pl.ds(rows - halo, halo)],
        dst_ref=halo_lo,
        send_sem=halo_send.at[1],
        recv_sem=halo_recv.at[1],
        device_id={"dom": lax.rem(me + 1, n)},
    )

    @pl.when(me > 0)
    def _():
        down.start()

    @pl.when(me < n - 1)
    def _():
        up.start()

    early_down = pltpu.make_async_remote_copy(
        src_ref=early_in.at[pl.ds(0, halo)],
        dst_ref=early_hi,
        send_sem=halo_send.at[2],
        recv_sem=halo_recv.at[2],
        device_id={"dom": lax.rem(me + n - 1, n)},
    )
    early_up = pltpu.make_async_remote_copy(
        src_ref=early_in.at[pl.ds(rows - halo, halo)],
        dst_ref=early_lo,
        send_sem=halo_send.at[3],
        recv_sem=halo_recv.at[3],
        device_id={"dom": lax.rem(me + 1, n)},
    )

    w_own = w_ref[pl.ds(pl.multiple_of(side * half, half), half), :]
    w_far = w_ref[pl.ds(pl.multiple_of((1 - side) * half, half), half), :]
    w_b[pl.ds(0, 3 * half), :] = right_form(w_own)
    w_b[pl.ds(3 * half, 3 * part), :] = right_form(w_far[part:, :])
    w_b[pl.ds(3 * half + 3 * part, 3 * part), :] = right_form(w_far[:part, :])
    sums[0] = jnp.zeros((BLK, half), F32)

    pass_on(main_copy)
    await_sibling(main_copy)

    def panel_form(p, _):
        hub_b[p] = right_form(hubs[pl.ds(pl.multiple_of(p * BLK, BLK), BLK), :])
        return 0

    lax.fori_loop(0, panels, panel_form, 0)
    hub_tiles_copy.wait()

    last_at = slots + tiles
    shift = blocks - REACH
    group = 16

    def hub_products(g, _):
        for u in range(group):
            t = g * group + u
            got = jnp.dot(left_form(tl[t]), hub_b[panels_ref[0, t]], preferred_element_type=F32)
            sums[t + 1] = got + sums[chain_ref[t]]
        return 0

    lax.fori_loop(0, slots // group, hub_products, 0)

    hop.wait_recv()
    hubs_early[pl.ds(base, hd), :] = hub_in[...]
    send_own(side_copy)
    early_copy(0).wait_recv()
    early_copy(pieces - 1).wait_recv()

    @pl.when(me > 0)
    def _():
        early_down.start()

    @pl.when(me < n - 1)
    def _():
        early_up.start()

    @pl.when(me > 0)
    def _():
        up.wait_recv()

    @pl.when(me == 0)
    def _():
        halo_lo[...] = jnp.zeros((halo, half), F32)

    @pl.when(me < n - 1)
    def _():
        down.wait_recv()

    @pl.when(me == n - 1)
    def _():
        halo_hi[...] = jnp.zeros((halo, half), F32)

    for b in range(REACH):
        ext_b[b] = right_form(halo_lo[pl.ds(b * BLK, BLK), :])
        ext_b[REACH + blocks + b] = right_form(halo_hi[pl.ds(b * BLK, BLK), :])
    loc_tiles_copy.wait()

    def loc_products(g, _):
        for u in range(group):
            t = g * group + u
            got = jnp.dot(left_form(tl[slots + t]), ext_b[jnp.maximum(cols_ref[0, t] - shift, 0)], preferred_element_type=F32)
            sums[slots + t + 1] = got + sums[chain_ref[slots + t]]
        return 0

    lax.fori_loop(0, tiles // group, loc_products, 0)

    per = chunk // BLK

    def chunk_rows(c):
        return pl.ds(pl.multiple_of(c * chunk, chunk), chunk)

    def agg_copy(c):
        return pltpu.make_async_remote_copy(
            src_ref=late.at[chunk_rows(c)],
            dst_ref=late_in.at[chunk_rows(c)],
            send_sem=agg_send.at[c],
            recv_sem=agg_recv.at[c],
            device_id=mate,
        )

    def st_copy(c):
        return pltpu.make_async_remote_copy(
            src_ref=st_out.at[c],
            dst_ref=st_in.at[c],
            send_sem=st_send.at[c],
            recv_sem=st_recv.at[c],
            device_id=mate,
        )

    def out_copy(c):
        return pltpu.make_async_copy(hid.at[chunk_rows(c)], out_ref.at[chunk_rows(c)], out_sem.at[c])

    def send_chunk(c, _):
        for u in range(per):
            r = c * per + u
            at = pl.ds(pl.multiple_of(r * BLK, BLK), BLK)
            got = sums[chain_ref[last_at + r]]
            agg[at, :] = got
            late[at, :] = got[:, :part]
        agg_copy(c).start()
        return 0

    lax.fori_loop(0, chunks, send_chunk, 0)

    pass_on(side_copy)

    for q in range(1, pieces - 1):
        early_copy(q).wait_recv()

    def own_early(b, _):
        ext_b[REACH + b, :, 0:part] = right_form(early_in[pl.ds(pl.multiple_of(b * BLK, BLK), BLK), :])
        return 0

    lax.fori_loop(0, blocks, own_early, 0)

    @pl.when(me > 0)
    def _():
        early_up.wait_recv()

    @pl.when(me == 0)
    def _():
        early_lo[...] = jnp.zeros((halo, part), F32)

    @pl.when(me < n - 1)
    def _():
        early_down.wait_recv()

    @pl.when(me == n - 1)
    def _():
        early_hi[...] = jnp.zeros((halo, part), F32)

    for b in range(REACH):
        ext_b[b, :, 0:part] = right_form(early_lo[pl.ds(b * BLK, BLK), :])
        ext_b[REACH + blocks + b, :, 0:part] = right_form(early_hi[pl.ds(b * BLK, BLK), :])

    await_sibling(side_copy)

    def hub_early(p, _):
        hub_b[p, :, 0:part] = right_form(hubs_early[pl.ds(pl.multiple_of(p * BLK, BLK), BLK), :])
        return 0

    lax.fori_loop(0, panels, hub_early, 0)

    def hub_products_early(g, _):
        for u in range(group):
            t = g * group + u
            right = hub_b[panels_ref[0, t], :, 0:part]
            got = jnp.dot(left_form(tl[t]), right, preferred_element_type=F32)
            sums[t + 1, :, 0:part] = got + sums[chain_ref[t], :, 0:part]
        return 0

    lax.fori_loop(0, slots // group, hub_products_early, 0)

    def loc_products_early(g, _):
        for u in range(group):
            t = g * group + u
            right = ext_b[jnp.maximum(cols_ref[0, t] - shift, 0), :, 0:part]
            got = jnp.dot(left_form(tl[slots + t]), right, preferred_element_type=F32)
            sums[slots + t + 1, :, 0:part] = got + sums[chain_ref[slots + t], :, 0:part]
        return 0

    lax.fori_loop(0, tiles // group, loc_products_early, 0)

    bias = bias_ref[...]
    width = 2.0 * half

    def finish(c):
        st_copy(c).wait_recv()
        both = st_out[c] + st_in[c]
        turned = jnp.concatenate([both] * (BLK // 8), axis=0).T
        mean = turned[:, 0:1] / width
        square = turned[:, 4:5] / width
        scale = lax.rsqrt(square - mean * mean + 1e-05)
        hid[chunk_rows(c), :] = (hid[chunk_rows(c), :] - mean) * scale
        out_copy(c).start()

    def mix(c, _):
        at = chunk_rows(c)
        got = jnp.concatenate([sums[chain_ref[last_at + c * per + u], :, 0:part] for u in range(per)], axis=0)
        left = jnp.concatenate([left_form(agg[at, :]), left_form(got)], axis=1)
        pre = jnp.dot(left, w_b[pl.ds(0, 3 * half + 3 * part), :], preferred_element_type=F32) + bias
        agg_copy(c).wait_recv()
        right = w_b[pl.ds(3 * half + 3 * part, 3 * part), :]
        pre = pre + jnp.dot(left_form(late_in[at, :]), right, preferred_element_type=F32)
        hidden = fil[at, :] + pre / (1.0 + jnp.exp(-pre))
        hid[at, :] = hidden
        one = jnp.sum(hidden, axis=1, keepdims=True)
        two = jnp.sum(hidden * hidden, axis=1, keepdims=True)
        lane = lax.broadcasted_iota(jnp.int32, (chunk, BLK), 1)
        packed = jnp.where(lax.rem(lane, 8) < 4, jnp.broadcast_to(one, (chunk, BLK)), jnp.broadcast_to(two, (chunk, BLK)))
        st_out[c] = packed.T[0:8, :]
        st_copy(c).start()

        @pl.when(c > 0)
        def _():
            finish(c - 1)

        return 0

    lax.fori_loop(0, chunks, mix, 0)
    finish(chunks - 1)

    def close(c, _):
        agg_copy(c).wait_send()
        st_copy(c).wait_send()
        out_copy(c).wait()
        return 0

    lax.fori_loop(0, chunks, close, 0)

    close_sends(main_copy)
    close_sends(side_copy)
    hop.wait_send()
    for q in range(pieces):
        early_copy(q).wait_send()

    @pl.when(me > 0)
    def _():
        down.wait_send()
        early_down.wait_send()

    @pl.when(me < n - 1)
    def _():
        up.wait_send()
        early_up.wait_send()


def shards(
    features,
    infill_mask,
    mask_token,
    local_rows,
    local_cols,
    local_tiles,
    hub_ids,
    hub_count,
    hub_rows,
    hub_panels,
    hub_tiles,
    mix_weight,
    mix_bias,
    norm_gain,
):
    rows, half = features.shape
    blocks = rows // BLK
    n = lax.axis_size("dom")
    hd = hub_ids.shape[0]
    tiles = local_rows.shape[1]
    slots = hub_rows.shape[1]
    chunk = 256
    chunks = rows // chunk
    i32 = jnp.int32

    live = jnp.arange(slots, dtype=i32) < hub_count[0]
    row_of = jnp.concatenate([jnp.where(live, hub_rows[0], -1), local_rows[0]])
    total = slots + tiles
    seq = jnp.arange(total, dtype=i32)
    target = jnp.concatenate([row_of, jnp.arange(blocks, dtype=i32)])
    limit = jnp.concatenate([seq, jnp.full((blocks,), total, i32)])
    same = (row_of[None, :] == target[:, None]) & (seq[None, :] < limit[:, None])
    chain = jnp.max(jnp.where(same, seq[None, :] + 1, 0), axis=1)

    vmem = pl.BlockSpec(memory_space=pltpu.VMEM)
    smem = pl.BlockSpec(memory_space=pltpu.SMEM)
    anym = pl.BlockSpec(memory_space=pl.ANY)
    dma = pltpu.SemaphoreType.DMA
    flops = 6 * BLK * BLK * half * total + 6 * rows * 2 * half * half
    part = half // 2
    halo = REACH * BLK
    pieces = rows // halo
    normed = pl.pallas_call(
        functools.partial(kernel, n, rows, half, hd, slots, tiles, chunk),
        out_shape=jax.ShapeDtypeStruct((rows, half), F32),
        in_specs=[anym, vmem, vmem, smem, smem, smem, smem, anym, anym, vmem, vmem],
        out_specs=anym,
        scratch_shapes=[
            pltpu.VMEM((rows, half), F32),
            pltpu.VMEM((REACH * BLK, half), F32),
            pltpu.VMEM((REACH * BLK, half), F32),
            pltpu.VMEM((rows, part), F32),
            pltpu.VMEM((rows, part), F32),
            pltpu.VMEM((halo, part), F32),
            pltpu.VMEM((halo, part), F32),
            pltpu.VMEM((hd, part), F32),
            pltpu.VMEM((hd, part), F32),
            pltpu.VMEM((n * hd, half), F32),
            pltpu.VMEM((n * hd, part), F32),
            pltpu.VMEM((blocks + 2 * REACH, 3 * BLK, half), BF16),
            pltpu.VMEM((n * hd // BLK, 3 * BLK, half), BF16),
            pltpu.VMEM((total, BLK, BLK), F32),
            pltpu.VMEM((total + 1, BLK, half), F32),
            pltpu.VMEM((rows, half), F32),
            pltpu.VMEM((rows, part), F32),
            pltpu.VMEM((rows, part), F32),
            pltpu.VMEM((rows, half), F32),
            pltpu.VMEM((6 * half, half), BF16),
            pltpu.VMEM((chunks, 8, chunk), F32),
            pltpu.VMEM((chunks, 8, chunk), F32),
            dma((2,)),
            dma((pieces,)),
            dma((pieces,)),
            dma((pieces,)),
            dma((1,)),
            dma((1,)),
            dma((n,)),
            dma((n,)),
            dma((n,)),
            dma((n,)),
            dma((4,)),
            dma((4,)),
            dma((chunks,)),
            dma((chunks,)),
            dma((chunks,)),
            dma((chunks,)),
            dma((chunks,)),
        ],
        compiler_params=pltpu.CompilerParams(
            collective_id=0, has_side_effects=True, vmem_limit_bytes=58 * 1024 * 1024
        ),
        cost_estimate=pl.CostEstimate(flops=flops, bytes_accessed=13 << 20, transcendentals=rows * half),
    )(
        features,
        infill_mask.reshape(blocks, BLK),
        mask_token[None, :],
        local_cols,
        hub_panels,
        hub_ids,
        chain,
        local_tiles[0],
        hub_tiles[0],
        mix_weight,
        mix_bias[None, :],
    )
    return normed * norm_gain[None, :]


def solution(mesh):
    in_specs = (
        P("dom", "feat"),
        P("dom"),
        P("feat"),
        P("dom", None),
        P("dom", None),
        P("dom", None, None, None),
        P("dom"),
        P("dom"),
        P("dom", None),
        P("dom", None),
        P("dom", None, None, None),
        P(None, "feat"),
        P("feat"),
        P("feat"),
    )
    out_specs = P("dom", "feat")
    return jax.shard_map(shards, mesh=mesh, in_specs=in_specs, out_specs=out_specs, check_vma=False)
```
